32 devices in a mesh: grp: 2 (over y), col: 4 (over z), row: 4 (over x, core).
Axes of the slice: x: 2, y: 2, z: 4, core: 2. Of those that a mesh axis runs over, the one named last changes fastest.
Arguments:
- records: float32 [32768, 1024], P(('grp', 'row'), 'col'), parts along dimension 0, may hold values from -90 to 90
Outputs:
- whitened: float32 [8, 4096, 1024], P(('grp', 'row'), 'col'), parts along dimension 0
The draws below stay inside these ranges and needn't reach their ends.
There are 2 independent parts, one for each index of `grp`. The reference program is written for one: setup_inputs(seed, part) draws one part's arguments, and reference() takes and returns one part's arrays. A program takes and returns all parts, laid end to end along the dimension named above; each array names one. Nothing has to cross between parts.
All inputs are finite; a program needn't handle non-finite values.
Results may differ from the reference program's by a relative error of at most 0.00022.
Values sent between devices are 32-bit elements; how exact they have to be, the bound alone decides.
A program may use at most 64 MiB of HBM per device.

```python
import math
import jax
import jax.numpy as jnp
from jax import lax

BLK = 128
ROWS_DEV = 4096
NS_ITERS = 8
TOURS = 2
ROWS = 16384
N = 1024
N_COL = 4
N_ROW = 4


def draw_records(key, part):
    subkeys = jax.random.split(key, 2)
    base_noise = jax.random.truncated_normal(subkeys[0], -4.0, 4.0, (ROWS, N), jnp.float32)
    blended = base_noise + 0.5 * jnp.roll(base_noise, 1, axis=1) - 0.3 * jnp.roll(base_noise, 3, axis=1)
    col_scale = jnp.exp(jax.random.uniform(subkeys[1], (1, N), jnp.float32, math.log(0.3), math.log(3.0)))
    row_scale = jnp.exp(math.log(10.0) * (jnp.arange(ROWS, dtype=jnp.float32) / ROWS - 0.5))[:, None]
    return blended * col_scale * row_scale


def setup_inputs(seed: int = 0, part: int = 0) -> dict:
    key_of = jax.random.split(jax.random.key(seed), 2)
    part_keys = jax.random.split(jax.random.fold_in(key_of[1], part), 2)
    records = draw_records(jax.random.fold_in(jax.random.fold_in(key_of[1], part), 71), part)
    return {"records": records}


def inverse_root(gram_pair):
    pair_width = gram_pair.shape[0]
    identity = jnp.eye(pair_width, dtype=jnp.float32)
    norm_total = jnp.sqrt(jnp.sum(gram_pair * gram_pair) + 1e-06)
    root_part = gram_pair / norm_total
    inverse_part = identity
    for repeat in range(NS_ITERS):
        middle = 1.5 * identity - 0.5 * jnp.dot(inverse_part, root_part, precision=lax.Precision.HIGHEST, preferred_element_type=jnp.float32)
        root_part = jnp.dot(root_part, middle, precision=lax.Precision.HIGHEST, preferred_element_type=jnp.float32)
        inverse_part = jnp.dot(middle, inverse_part, precision=lax.Precision.HIGHEST, preferred_element_type=jnp.float32)
    return (inverse_part, norm_total)

def advance(top_blocks, bottom_blocks, col_count):
    new_tops = jnp.concatenate([top_blocks[:, :1], bottom_blocks[:, :1], top_blocks[:, 1:col_count - 1]], axis=1)
    new_bottoms = jnp.concatenate([bottom_blocks[:, 1:], top_blocks[:, col_count - 1:]], axis=1)
    return (new_tops, new_bottoms)

def reference(records):
    blocks = records.reshape(ROWS, N_COL, 2, BLK)
    top_blocks = blocks[:, :, 0]
    bottom_blocks = blocks[:, :, 1]
    for repeat in range(TOURS):
        pair_cols = jnp.concatenate([top_blocks, bottom_blocks], axis=2)
        gram_pairs = jnp.einsum('rpi,rpj->pij', pair_cols, pair_cols, precision=lax.Precision.HIGHEST)
        inverses, norm_totals = jax.vmap(inverse_root)(gram_pairs)
        factors = jnp.sqrt(ROWS / norm_totals)
        rotated = jnp.einsum('rpi,pij->rpj', pair_cols, inverses, precision=lax.Precision.HIGHEST) * factors[None, :, None]
        top_blocks, bottom_blocks = advance(rotated[:, :, :BLK], rotated[:, :, BLK:], N_COL)
    whitened = jnp.stack([top_blocks, bottom_blocks], axis=2).reshape(N_ROW, ROWS_DEV, N)
    return whitened
```

```python
import jax
import jax.numpy as jnp
from jax import lax
from jax.experimental import pallas as pl
from jax.experimental.pallas import tpu as pltpu
from jax.sharding import PartitionSpec as P

NS_ITERS = 8
TOURS = 2
MESH = pl.DeviceIdType.MESH
F32 = jnp.float32
BF16 = jnp.bfloat16
ROWS_FIRST = (((0,), (0,)), ((), ()))
PLAIN = (((1,), (0,)), ((), ()))
SLOTS = (((0, 0), (1, 1)), ((0, 1), (2, 1)), ((1, 0), (3, 1)), ((2, 0), (3, 0)))
PLACES = ((0, 2), (4, 1), (6, 3), (7, 5))


def exact_dot(left, right):
    return jnp.dot(left, right, precision=lax.Precision.HIGHEST, preferred_element_type=F32)


def halves_of(value):
    high = value.astype(BF16)
    low = (value - high.astype(F32)).astype(BF16)
    return high, low


def split_dot(left, right, dims=PLAIN):
    left_high, left_low = left
    right_high, right_low = right

    def one(a, b):
        return lax.dot_general(a, b, dims, preferred_element_type=F32)

    return one(left_high, right_high) + (one(left_high, right_low) + one(left_low, right_high))


def identity_of(width):
    rows = lax.broadcasted_iota(jnp.int32, (width, width), 0)
    cols = lax.broadcasted_iota(jnp.int32, (width, width), 1)
    return jnp.where(rows == cols, 1.0, 0.0).astype(F32)


def norm_of(gram):
    total = jnp.sum(jnp.sum(gram * gram, axis=1, keepdims=True), axis=0, keepdims=True)
    return jnp.sqrt(total + 1e-06)


def newton(y_ref, z_ref, count):
    width = y_ref.shape[1]
    identity = identity_of(width)
    for i in range(count):
        middle = 1.5 * identity - 0.5 * y_ref[i]
        y_ref[i] = exact_dot(y_ref[i], middle)
        z_ref[i] = middle

    @pl.loop(1, NS_ITERS - 1)
    def _(step):
        middles = []
        for i in range(count):
            middles.append(1.5 * identity - 0.5 * exact_dot(z_ref[i], y_ref[i]))
        for i in range(count):
            y_ref[i] = exact_dot(y_ref[i], middles[i])
            z_ref[i] = exact_dot(middles[i], z_ref[i])

    for i in range(count):
        middle = 1.5 * identity - 0.5 * exact_dot(z_ref[i], y_ref[i])
        z_ref[i] = exact_dot(middle, z_ref[i])


def kernel(x_ref, out_ref, w, got, ex, g, ga, sb, gb, gf, y1, z1, dg, dq, df, part, rs, zb, cq, cf, y2, z2,
           send_sem, recv_sem):
    n_col, n_row = 4, 4
    c = lax.axis_index("col")
    r = lax.axis_index("row")
    slab, width = x_ref.shape
    half = width // 2
    rows = slab // n_col
    quarter = half // n_row
    total_rows = float(slab * n_row)

    def col_peer(k):
        return {"col": lax.rem(c + k, n_col)}

    def row_peer(k):
        return {"row": lax.rem(r + k, n_row)}

    def remote(src, dst, sem, device):
        copy = pltpu.make_async_remote_copy(
            src_ref=src, dst_ref=dst, send_sem=send_sem.at[sem], recv_sem=recv_sem.at[sem],
            device_id=device, device_id_type=MESH)
        copy.start()
        return copy

    barrier = pltpu.get_barrier_semaphore()
    for k in range(1, n_row):
        pl.semaphore_signal(barrier, inc=1, device_id=row_peer(k), device_id_type=MESH)
    for k in range(1, n_col):
        pl.semaphore_signal(barrier, inc=1, device_id=col_peer(k), device_id_type=MESH)

    tile = 512
    g[...] = jnp.zeros_like(g)

    @pl.loop(0, slab // tile)
    def _(t):
        piece = halves_of(x_ref[pl.ds(pl.multiple_of(t * tile, tile), tile), :])
        g[...] += split_dot(piece, piece, ROWS_FIRST)

    pl.semaphore_wait(barrier, n_row + n_col - 2)

    core = lax.rem(r, 2)
    mine = pl.ds(pl.multiple_of(core * half, half), half)
    other = pl.ds(pl.multiple_of((1 - core) * half, half), half)
    core_peer = {"row": r + 1 - 2 * core}
    copy = remote(g.at[other], ga, 0, core_peer)
    copy.wait()
    sb[...] = g[mine, :] + ga[...]
    copy = remote(sb, gb, 1, row_peer(2))
    copy.wait()
    gf[mine, :] = sb[...] + gb[...]
    copy = remote(gf.at[mine], gf.at[mine], 2, core_peer)
    copy.wait()

    norm = norm_of(gf[...])
    y1[0] = gf[...] / norm
    newton(y1, z1, 1)
    z1[0] = z1[0] * jnp.sqrt(total_rows / norm)

    odd = lax.rem(c, 2)
    side = c // 2
    hx = 1 - odd * (1 - side)
    ho = 1 - hx
    partner = c + 1 - 2 * odd
    partner_far = lax.rem(partner + 2, n_col)
    far = lax.rem(c + 2, n_col)
    far_other = lax.rem(partner + 2, n_col)

    def chunk(j):
        return pl.ds(pl.multiple_of(j * rows, rows), rows)

    piece_rows = min(256, rows)

    def rotate(j):
        @pl.loop(0, rows // piece_rows)
        def _(t):
            at = pl.ds(pl.multiple_of(j * rows + t * piece_rows, piece_rows), piece_rows)
            turned = split_dot(halves_of(x_ref[at, :]), halves_of(z1[0]))
            w[0, at, :] = turned[:, :half]
            w[1, at, :] = turned[:, half:]

    first = []
    for k in (2, 3, 1):
        j = lax.rem(c + k, n_col)
        rotate(j)
        first.append(remote(w.at[hx, chunk(j)], got.at[c, hx], 2 + k, {"col": j}))
    first.append(remote(w.at[ho, chunk(partner)], got.at[c, ho], 6, {"col": partner}))
    first.append(remote(w.at[ho, chunk(partner_far)], ex.at[odd], 7, {"col": partner}))

    turned_gram = exact_dot(exact_dot(z1[0], gf[...]), z1[0])
    dg[0] = turned_gram[:half, :half]
    dg[1] = turned_gram[half:, half:]
    strip = pl.ds(pl.multiple_of(r * quarter, quarter), quarter)
    diagonal = []
    for k in (1, 2, 3):
        diagonal.append(remote(dg.at[:, strip], dq.at[c], 7 + k, col_peer(k)))
    dq[c] = dg[:, strip, :]

    rotate(c)
    got[c, 0] = w[0, chunk(c), :]
    got[c, 1] = w[1, chunk(c), :]
    ex[odd] = w[ho, chunk(far), :]

    for copy in diagonal:
        copy.wait()
    for k in (1, 2, 3):
        diagonal.append(remote(dq, df.at[r], 10 + k, row_peer(k)))
    df[r] = dq[...]
    for copy in diagonal[3:]:
        copy.wait()

    for copy in first:
        copy.wait_send()
    second = [
        remote(w.at[ho, chunk(far)], got.at[c, ho], 14, {"col": far}),
        remote(w.at[ho, chunk(far_other)], got.at[c, ho], 15, {"col": far_other}),
    ]
    for copy in first:
        copy.wait_recv()

    def cross(left, right):
        return split_dot(halves_of(left), halves_of(right), ROWS_FIRST)

    left_col = 2 * side
    part[...] = jnp.zeros_like(part)

    @pl.loop(0, rows // piece_rows)
    def _(t):
        at = pl.ds(pl.multiple_of(t * piece_rows, piece_rows), piece_rows)
        part[0] += cross(got[0, 1, at, :], got[2, 1, at, :])
        part[1] += cross(got[1, 0, at, :], got[3, 1, at, :])
        part[2] += cross(got[left_col, 0, at, :], got[left_col + 1, 1 - side, at, :])
        part[2] += cross(ex[0, at, :], ex[1, at, :])

    copies = []
    for k in (1, 2, 3):
        q = lax.rem(r + k, n_row)
        theirs = pl.ds(pl.multiple_of(q * quarter, quarter), quarter)
        copies.append(remote(part.at[:, theirs], rs.at[k - 1], 15 + k, {"row": q}))
    for copy in copies:
        copy.wait()
    zb[c] = (part[:, strip, :] + rs[0]) + (rs[1] + rs[2])
    copies = [remote(zb.at[c], zb.at[c], 18 + k, col_peer(k)) for k in (1, 2, 3)]
    for copy in copies:
        copy.wait()
    cq[0] = zb[0, 2] + zb[1, 2]
    cq[1] = (zb[0, 0] + zb[1, 0]) + (zb[2, 0] + zb[3, 0])
    cq[2] = (zb[0, 1] + zb[1, 1]) + (zb[2, 1] + zb[3, 1])
    cq[3] = zb[2, 2] + zb[3, 2]
    copies = [remote(cq, cf.at[r], 21 + k, row_peer(k)) for k in (1, 2, 3)]
    cf[r] = cq[...]
    for copy in copies:
        copy.wait()

    factors = []
    for slot, ((lc, lh), (rc, rh)) in enumerate(SLOTS):
        for q in range(n_row):
            at = slice(q * quarter, (q + 1) * quarter)
            low = slice(half + q * quarter, half + (q + 1) * quarter)
            y2[slot, at, :half] = df[q, lc, lh]
            y2[slot, low, half:] = df[q, rc, rh]
            y2[slot, at, half:] = cf[q, slot]
        y2[slot, half:, :half] = jnp.transpose(y2[slot, :half, half:])
        gram = y2[slot]
        norm = norm_of(gram)
        y2[slot] = gram / norm
        factors.append(jnp.sqrt(total_rows / norm))
    newton(y2, z2, 4)
    for slot in range(4):
        z2[slot] = z2[slot] * factors[slot]

    def finish(slot):
        (lc, lh), (rc, rh) = SLOTS[slot]

        @pl.loop(0, rows // piece_rows)
        def _(t):
            at = pl.ds(pl.multiple_of(t * piece_rows, piece_rows), piece_rows)
            both = jnp.concatenate([got[lc, lh, at, :], got[rc, rh, at, :]], axis=1)
            turned = split_dot(halves_of(both), halves_of(z2[slot]))
            for side_of in range(2):
                place = PLACES[slot][side_of]
                out_ref[at, place * half:(place + 1) * half] = turned[:, side_of * half:(side_of + 1) * half]

    finish(1)
    finish(2)
    for copy in second:
        copy.wait()
    finish(0)
    finish(3)


def fused(records):
    slab, width = records.shape
    half = width // 2
    rows = slab // 4
    quarter = half // 4
    out = pl.pallas_call(
        kernel,
        out_shape=jax.ShapeDtypeStruct((rows, 4 * width), F32),
        in_specs=[pl.BlockSpec(memory_space=pltpu.VMEM)],
        out_specs=pl.BlockSpec(memory_space=pltpu.VMEM),
        scratch_shapes=[
            pltpu.VMEM((2, slab, half), F32),
            pltpu.VMEM((4, 2, rows, half), F32),
            pltpu.VMEM((2, rows, half), F32),
            pltpu.VMEM((width, width), F32),
            pltpu.VMEM((half, width), F32),
            pltpu.VMEM((half, width), F32),
            pltpu.VMEM((half, width), F32),
            pltpu.VMEM((width, width), F32),
            pltpu.VMEM((1, width, width), F32),
            pltpu.VMEM((1, width, width), F32),
            pltpu.VMEM((2, half, half), F32),
            pltpu.VMEM((4, 2, quarter, half), F32),
            pltpu.VMEM((4, 4, 2, quarter, half), F32),
            pltpu.VMEM((3, half, half), F32),
            pltpu.VMEM((3, 3, quarter, half), F32),
            pltpu.VMEM((4, 3, quarter, half), F32),
            pltpu.VMEM((4, quarter, half), F32),
            pltpu.VMEM((4, 4, quarter, half), F32),
            pltpu.VMEM((4, width, width), F32),
            pltpu.VMEM((4, width, width), F32),
            pltpu.SemaphoreType.DMA((25,)),
            pltpu.SemaphoreType.DMA((25,)),
        ],
        compiler_params=pltpu.CompilerParams(
            collective_id=0, has_side_effects=True, vmem_limit_bytes=48 * 1024 * 1024),
    )(records)
    return out.reshape(1, rows, 4 * width)


def shifted(x, axis, by):
    peers = lax.axis_size(axis)
    pairs = [(i, i + by) for i in range(peers) if 0 <= i + by < peers]
    return lax.ppermute(x, axis, pairs)


def local_gram(left, right):
    return lax.dot_general(
        left, right, ROWS_FIRST, precision=lax.Precision.HIGHEST, preferred_element_type=F32)


def inverse_root(gram_pair):
    identity = jnp.eye(gram_pair.shape[0], dtype=F32)
    norm_total = jnp.sqrt(jnp.sum(gram_pair * gram_pair) + 1e-06)
    root_part = gram_pair / norm_total
    inverse_part = identity
    for repeat in range(NS_ITERS):
        middle = 1.5 * identity - 0.5 * exact_dot(inverse_part, root_part)
        root_part = exact_dot(root_part, middle)
        inverse_part = exact_dot(middle, inverse_part)
    return (inverse_part, norm_total)


def stepwise(records):
    col_count = lax.axis_size("col")
    total_rows = records.shape[0] * lax.axis_size("row")
    position = lax.axis_index("col")
    first_col = position == 0
    last_col = position == col_count - 1
    block_width = records.shape[1] // 2
    pair_cols = records
    for repeat in range(TOURS):
        gram_pair = lax.psum(local_gram(pair_cols, pair_cols), "row")
        inverse_part, norm_total = inverse_root(gram_pair)
        factor = jnp.sqrt(total_rows / norm_total)
        pair_cols = exact_dot(pair_cols, inverse_part) * factor
        top_block = pair_cols[:, :block_width]
        bottom_block = pair_cols[:, block_width:]
        outgoing = jnp.where(first_col, bottom_block, top_block)
        arrived = shifted(outgoing, "col", 1)
        returned = shifted(bottom_block, "col", -1)
        new_bottom = jnp.where(last_col, top_block, returned)
        top_block = jnp.where(first_col, top_block, arrived)
        pair_cols = jnp.concatenate([top_block, new_bottom], axis=1)
    spread = lax.all_to_all(pair_cols, "col", split_axis=0, concat_axis=1, tiled=True)
    return spread.reshape(1, spread.shape[0], spread.shape[1])


def solution(mesh):
    placed = (P(("grp", "row"), "col"),)
    small = mesh.shape["col"] == 4 and mesh.shape["row"] == 4
    return jax.shard_map(
        fused if small else stepwise,
        mesh=mesh, in_specs=placed, out_specs=P(("grp", "row"), "col", None), check_vma=False
    )
```

```python
import jax
import jax.numpy as jnp
from jax import lax
from jax.experimental import pallas as pl
from jax.experimental.pallas import tpu as pltpu
from jax.sharding import PartitionSpec as P

NS_ITERS = 8
TOURS = 2
MESH = pl.DeviceIdType.MESH
F32 = jnp.float32
BF16 = jnp.bfloat16
ROWS_FIRST = (((0,), (0,)), ((), ()))
PLAIN = (((1,), (0,)), ((), ()))
SLOTS = (((0, 0), (1, 1)), ((0, 1), (2, 1)), ((1, 0), (3, 1)), ((2, 0), (3, 0)))
PLACES = ((0, 2), (4, 1), (6, 3), (7, 5))


def exact_dot(left, right):
    return jnp.dot(left, right, precision=lax.Precision.HIGHEST, preferred_element_type=F32)


def halves_of(value):
    high = value.astype(BF16)
    low = (value - high.astype(F32)).astype(BF16)
    return high, low


def split_dot(left, right, dims=PLAIN):
    left_high, left_low = left
    right_high, right_low = right

    def one(a, b):
        return lax.dot_general(a, b, dims, preferred_element_type=F32)

    return one(left_high, right_high) + (one(left_high, right_low) + one(left_low, right_high))


def identity_of(width):
    rows = lax.broadcasted_iota(jnp.int32, (width, width), 0)
    cols = lax.broadcasted_iota(jnp.int32, (width, width), 1)
    return jnp.where(rows == cols, 1.0, 0.0).astype(F32)


def norm_of(gram):
    total = jnp.sum(jnp.sum(gram * gram, axis=1, keepdims=True), axis=0, keepdims=True)
    return jnp.sqrt(total + 1e-06)


def newton(y_ref, z_ref, count):
    width = y_ref.shape[1]
    identity = identity_of(width)
    for i in range(count):
        middle = 1.5 * identity - 0.5 * y_ref[i]
        y_ref[i] = exact_dot(y_ref[i], middle)
        z_ref[i] = middle

    @pl.loop(1, NS_ITERS - 1)
    def _(step):
        middles = []
        for i in range(count):
            middles.append(1.5 * identity - 0.5 * exact_dot(z_ref[i], y_ref[i]))
        for i in range(count):
            y_ref[i] = exact_dot(y_ref[i], middles[i])
            z_ref[i] = exact_dot(middles[i], z_ref[i])

    for i in range(count):
        middle = 1.5 * identity - 0.5 * exact_dot(z_ref[i], y_ref[i])
        z_ref[i] = exact_dot(middle, z_ref[i])


def kernel(x_ref, out_ref, w, got, ex, g, ga, sb, gb, gf, y1, z1, dg, dq, df, part, rs, zb, cq, cf, y2, z2,
           send_sem, recv_sem):
    n_col, n_row = 4, 4
    c = lax.axis_index("col")
    r = lax.axis_index("row")
    slab, width = x_ref.shape
    half = width // 2
    rows = slab // n_col
    quarter = half // n_row
    total_rows = float(slab * n_row)

    def col_peer(k):
        return {"col": lax.rem(c + k, n_col)}

    def row_peer(k):
        return {"row": lax.rem(r + k, n_row)}

    def remote(src, dst, sem, device):
        copy = pltpu.make_async_remote_copy(
            src_ref=src, dst_ref=dst, send_sem=send_sem.at[sem], recv_sem=recv_sem.at[sem],
            device_id=device, device_id_type=MESH)
        copy.start()
        return copy

    barrier = pltpu.get_barrier_semaphore()
    for k in range(1, n_row):
        pl.semaphore_signal(barrier, inc=1, device_id=row_peer(k), device_id_type=MESH)
    for k in range(1, n_col):
        pl.semaphore_signal(barrier, inc=1, device_id=col_peer(k), device_id_type=MESH)

    tile = 512
    g[...] = jnp.zeros_like(g)
    gf[...] = jnp.zeros_like(gf)

    @pl.loop(0, slab // tile)
    def _(t):
        piece = halves_of(x_ref[pl.ds(pl.multiple_of(t * tile, tile), tile), :])
        g[...] += lax.dot_general(piece[0], piece[0], ROWS_FIRST, preferred_element_type=F32)
        gf[...] += lax.dot_general(piece[0], piece[1], ROWS_FIRST, preferred_element_type=F32)

    g[...] += gf[...] + jnp.transpose(gf[...])

    pl.semaphore_wait(barrier, n_row + n_col - 2)

    core = lax.rem(r, 2)
    mine = pl.ds(pl.multiple_of(core * half, half), half)
    other = pl.ds(pl.multiple_of((1 - core) * half, half), half)
    core_peer = {"row": r + 1 - 2 * core}
    copy = remote(g.at[other], ga, 0, core_peer)
    copy.wait()
    sb[...] = g[mine, :] + ga[...]
    copy = remote(sb, gb, 1, row_peer(2))
    copy.wait()
    gf[mine, :] = sb[...] + gb[...]
    copy = remote(gf.at[mine], gf.at[mine], 2, core_peer)
    copy.wait()

    norm = norm_of(gf[...])
    y1[0] = gf[...] / norm
    newton(y1, z1, 1)
    z1[0] = z1[0] * jnp.sqrt(total_rows / norm)

    odd = lax.rem(c, 2)
    side = c // 2
    hx = 1 - odd * (1 - side)
    ho = 1 - hx
    partner = c + 1 - 2 * odd
    far = lax.rem(c + 2, n_col)
    far_other = lax.rem(partner + 2, n_col)

    def chunk(j):
        return pl.ds(pl.multiple_of(j * rows, rows), rows)

    piece_rows = min(256, rows)

    def rotate(j):
        @pl.loop(0, rows // piece_rows)
        def _(t):
            at = pl.ds(pl.multiple_of(j * rows + t * piece_rows, piece_rows), piece_rows)
            turned = split_dot(halves_of(x_ref[at, :]), halves_of(z1[0]))
            w[0, at, :] = turned[:, :half]
            w[1, at, :] = turned[:, half:]

    rotate(far)
    crossing = [remote(w.at[hx, chunk(far)], got.at[c, hx], 3, {"col": far})]

    turned_gram = exact_dot(exact_dot(z1[0], gf[...]), z1[0])
    dg[0] = turned_gram[:half, :half]
    dg[1] = turned_gram[half:, half:]
    strip = pl.ds(pl.multiple_of(r * quarter, quarter), quarter)
    diagonal = []
    for k in (1, 2, 3):
        diagonal.append(remote(dg.at[:, strip], dq.at[c], 7 + k, col_peer(k)))
    dq[c] = dg[:, strip, :]

    rotate(far_other)
    crossing.append(remote(w.at[hx, chunk(far_other)], got.at[c, hx], 4, {"col": far_other}))
    near = [remote(w.at[ho, chunk(far_other)], ex.at[odd], 7, {"col": partner})]
    rotate(partner)
    near.append(remote(w.at[hx, chunk(partner)], got.at[c, hx], 5, {"col": partner}))
    near.append(remote(w.at[ho, chunk(partner)], got.at[c, ho], 6, {"col": partner}))

    rotate(c)
    got[c, 0] = w[0, chunk(c), :]
    got[c, 1] = w[1, chunk(c), :]
    ex[odd] = w[ho, chunk(far), :]

    def later(part_of, sem):
        size = rows // 2
        sent = []
        for i, j in enumerate((far, far_other)):
            at = pl.ds(pl.multiple_of(j * rows + part_of * size, size), size)
            to = pl.ds(part_of * size, size)
            sent.append(remote(w.at[ho, at], got.at[c, ho, to], sem + i, {"col": j}))
        return sent

    for copy in crossing:
        copy.wait_send()
    second = later(0, 14)

    for copy in diagonal:
        copy.wait()
    for k in (1, 2, 3):
        diagonal.append(remote(dq, df.at[r], 10 + k, row_peer(k)))
    df[r] = dq[...]
    for copy in diagonal[3:]:
        copy.wait()
    for copy in crossing:
        copy.wait_recv()
    for copy in near:
        copy.wait()

    def cross(left, right):
        return split_dot(halves_of(left), halves_of(right), ROWS_FIRST)

    left_col = 2 * side
    part[...] = jnp.zeros_like(part)

    @pl.loop(0, rows // piece_rows)
    def _(t):
        at = pl.ds(pl.multiple_of(t * piece_rows, piece_rows), piece_rows)
        part[0] += cross(got[0, 1, at, :], got[2, 1, at, :])
        part[1] += cross(got[1, 0, at, :], got[3, 1, at, :])
        part[2] += cross(got[left_col, 0, at, :], got[left_col + 1, 1 - side, at, :])
        part[2] += cross(ex[0, at, :], ex[1, at, :])

    copies = []
    for k in (1, 2, 3):
        q = lax.rem(r + k, n_row)
        theirs = pl.ds(pl.multiple_of(q * quarter, quarter), quarter)
        copies.append(remote(part.at[:, theirs], rs.at[k - 1], 15 + k, {"row": q}))
    for copy in copies:
        copy.wait()
    zb[c] = (part[:, strip, :] + rs[0]) + (rs[1] + rs[2])
    copies = [remote(zb.at[c], zb.at[c], 18 + k, col_peer(k)) for k in (1, 2, 3)]
    second += later(1, 25)
    for copy in copies:
        copy.wait()
    cq[0] = zb[0, 2] + zb[1, 2]
    cq[1] = (zb[0, 0] + zb[1, 0]) + (zb[2, 0] + zb[3, 0])
    cq[2] = (zb[0, 1] + zb[1, 1]) + (zb[2, 1] + zb[3, 1])
    cq[3] = zb[2, 2] + zb[3, 2]
    copies = [remote(cq, cf.at[r], 21 + k, row_peer(k)) for k in (1, 2, 3)]
    cf[r] = cq[...]
    for copy in copies:
        copy.wait()

    for slot, ((lc, lh), (rc, rh)) in enumerate(SLOTS):
        for q in range(n_row):
            at = slice(q * quarter, (q + 1) * quarter)
            low = slice(half + q * quarter, half + (q + 1) * quarter)
            y2[slot, at, :half] = df[q, lc, lh]
            y2[slot, low, half:] = df[q, rc, rh]
            y2[slot, at, half:] = cf[q, slot]
        y2[slot, half:, :half] = jnp.transpose(y2[slot, :half, half:])

    factors = []
    for i in range(2):
        gram = y2[2 * core + i]
        norm = norm_of(gram)
        y2[2 * core + i] = gram / norm
        factors.append(jnp.sqrt(total_rows / norm))
    own = pl.ds(2 * core, 2)
    newton(y2.at[own], z2.at[own], 2)
    for i in range(2):
        z2[2 * core + i] = z2[2 * core + i] * factors[i]
    copy = remote(z2.at[own], z2.at[own], 27, core_peer)
    copy.wait()

    def finish(slot):
        (lc, lh), (rc, rh) = SLOTS[slot]

        @pl.loop(0, rows // piece_rows)
        def _(t):
            at = pl.ds(pl.multiple_of(t * piece_rows, piece_rows), piece_rows)
            both = jnp.concatenate([got[lc, lh, at, :], got[rc, rh, at, :]], axis=1)
            turned = split_dot(halves_of(both), halves_of(z2[slot]))
            for side_of in range(2):
                place = PLACES[slot][side_of]
                out_ref[at, place * half:(place + 1) * half] = turned[:, side_of * half:(side_of + 1) * half]

    finish(1)
    finish(2)
    for copy in second:
        copy.wait()
    finish(0)
    finish(3)


def fused(records):
    slab, width = records.shape
    half = width // 2
    rows = slab // 4
    quarter = half // 4
    out = pl.pallas_call(
        kernel,
        out_shape=jax.ShapeDtypeStruct((rows, 4 * width), F32),
        in_specs=[pl.BlockSpec(memory_space=pltpu.VMEM)],
        out_specs=pl.BlockSpec(memory_space=pltpu.VMEM),
        scratch_shapes=[
            pltpu.VMEM((2, slab, half), F32),
            pltpu.VMEM((4, 2, rows, half), F32),
            pltpu.VMEM((2, rows, half), F32),
            pltpu.VMEM((width, width), F32),
            pltpu.VMEM((half, width), F32),
            pltpu.VMEM((half, width), F32),
            pltpu.VMEM((half, width), F32),
            pltpu.VMEM((width, width), F32),
            pltpu.VMEM((1, width, width), F32),
            pltpu.VMEM((1, width, width), F32),
            pltpu.VMEM((2, half, half), F32),
            pltpu.VMEM((4, 2, quarter, half), F32),
            pltpu.VMEM((4, 4, 2, quarter, half), F32),
            pltpu.VMEM((3, half, half), F32),
            pltpu.VMEM((3, 3, quarter, half), F32),
            pltpu.VMEM((4, 3, quarter, half), F32),
            pltpu.VMEM((4, quarter, half), F32),
            pltpu.VMEM((4, 4, quarter, half), F32),
            pltpu.VMEM((4, width, width), F32),
            pltpu.VMEM((4, width, width), F32),
            pltpu.SemaphoreType.DMA((28,)),
            pltpu.SemaphoreType.DMA((28,)),
        ],
        compiler_params=pltpu.CompilerParams(
            collective_id=0, has_side_effects=True, vmem_limit_bytes=48 * 1024 * 1024),
    )(records)
    return out.reshape(1, rows, 4 * width)


def shifted(x, axis, by):
    peers = lax.axis_size(axis)
    pairs = [(i, i + by) for i in range(peers) if 0 <= i + by < peers]
    return lax.ppermute(x, axis, pairs)


def local_gram(left, right):
    return lax.dot_general(
        left, right, ROWS_FIRST, precision=lax.Precision.HIGHEST, preferred_element_type=F32)


def inverse_root(gram_pair):
    identity = jnp.eye(gram_pair.shape[0], dtype=F32)
    norm_total = jnp.sqrt(jnp.sum(gram_pair * gram_pair) + 1e-06)
    root_part = gram_pair / norm_total
    inverse_part = identity
    for repeat in range(NS_ITERS):
        middle = 1.5 * identity - 0.5 * exact_dot(inverse_part, root_part)
        root_part = exact_dot(root_part, middle)
        inverse_part = exact_dot(middle, inverse_part)
    return (inverse_part, norm_total)


def stepwise(records):
    col_count = lax.axis_size("col")
    total_rows = records.shape[0] * lax.axis_size("row")
    position = lax.axis_index("col")
    first_col = position == 0
    last_col = position == col_count - 1
    block_width = records.shape[1] // 2
    pair_cols = records
    for repeat in range(TOURS):
        gram_pair = lax.psum(local_gram(pair_cols, pair_cols), "row")
        inverse_part, norm_total = inverse_root(gram_pair)
        factor = jnp.sqrt(total_rows / norm_total)
        pair_cols = exact_dot(pair_cols, inverse_part) * factor
        top_block = pair_cols[:, :block_width]
        bottom_block = pair_cols[:, block_width:]
        outgoing = jnp.where(first_col, bottom_block, top_block)
        arrived = shifted(outgoing, "col", 1)
        returned = shifted(bottom_block, "col", -1)
        new_bottom = jnp.where(last_col, top_block, returned)
        top_block = jnp.where(first_col, top_block, arrived)
        pair_cols = jnp.concatenate([top_block, new_bottom], axis=1)
    spread = lax.all_to_all(pair_cols, "col", split_axis=0, concat_axis=1, tiled=True)
    return spread.reshape(1, spread.shape[0], spread.shape[1])


def solution(mesh):
    placed = (P(("grp", "row"), "col"),)
    small = mesh.shape["col"] == 4 and mesh.shape["row"] == 4
    return jax.shard_map(
        fused if small else stepwise,
        mesh=mesh, in_specs=placed, out_specs=P(("grp", "row"), "col", None), check_vma=False
    )
```

```python
import jax
import jax.numpy as jnp
from jax import lax
from jax.experimental import pallas as pl
from jax.experimental.pallas import tpu as pltpu
from jax.sharding import PartitionSpec as P

NS_ITERS = 8
TOURS = 2
MESH = pl.DeviceIdType.MESH
F32 = jnp.float32
BF16 = jnp.bfloat16
ROWS_FIRST = (((0,), (0,)), ((), ()))
PLAIN = (((1,), (0,)), ((), ()))
SLOTS = (((0, 0), (1, 1)), ((0, 1), (2, 1)), ((1, 0), (3, 1)), ((2, 0), (3, 0)))
PLACES = ((0, 2), (4, 1), (6, 3), (7, 5))


def exact_dot(left, right):
    return jnp.dot(left, right, precision=lax.Precision.HIGHEST, preferred_element_type=F32)


def halves_of(value):
    high = value.astype(BF16)
    low = (value - high.astype(F32)).astype(BF16)
    return high, low


def split_dot(left, right, dims=PLAIN):
    left_high, left_low = left
    right_high, right_low = right

    def one(a, b):
        return lax.dot_general(a, b, dims, preferred_element_type=F32)

    return one(left_high, right_high) + (one(left_high, right_low) + one(left_low, right_high))


def identity_of(width):
    rows = lax.broadcasted_iota(jnp.int32, (width, width), 0)
    cols = lax.broadcasted_iota(jnp.int32, (width, width), 1)
    return jnp.where(rows == cols, 1.0, 0.0).astype(F32)


def norm_of(gram):
    total = jnp.sum(jnp.sum(gram * gram, axis=1, keepdims=True), axis=0, keepdims=True)
    return jnp.sqrt(total + 1e-06)


def newton(y_ref, z_ref, count):
    width = y_ref.shape[1]
    identity = identity_of(width)
    for i in range(count):
        middle = 1.5 * identity - 0.5 * y_ref[i]
        y_ref[i] = exact_dot(y_ref[i], middle)
        z_ref[i] = middle

    @pl.loop(1, NS_ITERS - 1)
    def _(step):
        middles = []
        for i in range(count):
            middles.append(1.5 * identity - 0.5 * exact_dot(z_ref[i], y_ref[i]))
        for i in range(count):
            y_ref[i] = exact_dot(y_ref[i], middles[i])
            z_ref[i] = exact_dot(middles[i], z_ref[i])

    for i in range(count):
        middle = 1.5 * identity - 0.5 * exact_dot(z_ref[i], y_ref[i])
        z_ref[i] = exact_dot(middle, z_ref[i])


def kernel(x_any, out_ref, x_ref, w, got, ex, g, ga, sb, gb, gf, y1, z1, dg, dq, df, part, rs, zb, cq, cf, y2, z2,
           send_sem, recv_sem, load_sem):
    n_col, n_row = 4, 4
    c = lax.axis_index("col")
    r = lax.axis_index("row")
    slab, width = x_ref.shape
    half = width // 2
    rows = slab // n_col
    quarter = half // n_row
    total_rows = float(slab * n_row)

    def col_peer(k):
        return {"col": lax.rem(c + k, n_col)}

    def row_peer(k):
        return {"row": lax.rem(r + k, n_row)}

    def remote(src, dst, sem, device):
        copy = pltpu.make_async_remote_copy(
            src_ref=src, dst_ref=dst, send_sem=send_sem.at[sem], recv_sem=recv_sem.at[sem],
            device_id=device, device_id_type=MESH)
        copy.start()
        return copy

    tile = slab // 8

    def load(t):
        at = pl.ds(pl.multiple_of(t * tile, tile), tile)
        return pltpu.make_async_copy(x_any.at[at], x_ref.at[at], load_sem.at[t])

    for t in range(8):
        load(t).start()

    barrier = pltpu.get_barrier_semaphore()
    for k in range(1, n_row):
        pl.semaphore_signal(barrier, inc=1, device_id=row_peer(k), device_id_type=MESH)
    for k in range(1, n_col):
        pl.semaphore_signal(barrier, inc=1, device_id=col_peer(k), device_id_type=MESH)

    g[...] = jnp.zeros_like(g)
    gf[...] = jnp.zeros_like(gf)

    @pl.loop(0, slab // tile)
    def _(t):
        load(t).wait()
        piece = halves_of(x_ref[pl.ds(pl.multiple_of(t * tile, tile), tile), :])
        g[...] += lax.dot_general(piece[0], piece[0], ROWS_FIRST, preferred_element_type=F32)
        gf[...] += lax.dot_general(piece[0], piece[1], ROWS_FIRST, preferred_element_type=F32)

    g[...] += gf[...] + jnp.transpose(gf[...])

    pl.semaphore_wait(barrier, n_row + n_col - 2)

    core = lax.rem(r, 2)
    mine = pl.ds(pl.multiple_of(core * half, half), half)
    other = pl.ds(pl.multiple_of((1 - core) * half, half), half)
    core_peer = {"row": r + 1 - 2 * core}
    copy = remote(g.at[other], ga, 0, core_peer)
    copy.wait()
    sb[...] = g[mine, :] + ga[...]
    copy = remote(sb, gb, 1, row_peer(2))
    copy.wait()
    gf[mine, :] = sb[...] + gb[...]
    copy = remote(gf.at[mine], gf.at[mine], 2, core_peer)
    copy.wait()

    norm = norm_of(gf[...])
    y1[0] = gf[...] / norm
    newton(y1, z1, 1)
    z1[0] = z1[0] * jnp.sqrt(total_rows / norm)

    odd = lax.rem(c, 2)
    side = c // 2
    hx = 1 - odd * (1 - side)
    ho = 1 - hx
    partner = c + 1 - 2 * odd
    far = lax.rem(c + 2, n_col)
    far_other = lax.rem(partner + 2, n_col)

    def chunk(j):
        return pl.ds(pl.multiple_of(j * rows, rows), rows)

    piece_rows = min(256, rows)

    def rotate(j):
        @pl.loop(0, rows // piece_rows)
        def _(t):
            at = pl.ds(pl.multiple_of(j * rows + t * piece_rows, piece_rows), piece_rows)
            turned = split_dot(halves_of(x_ref[at, :]), halves_of(z1[0]))
            w[0, at, :] = turned[:, :half]
            w[1, at, :] = turned[:, half:]

    rotate(far)
    crossing = [remote(w.at[hx, chunk(far)], got.at[c, hx], 3, {"col": far})]

    turned_gram = exact_dot(exact_dot(z1[0], gf[...]), z1[0])
    dg[0] = turned_gram[:half, :half]
    dg[1] = turned_gram[half:, half:]
    strip = pl.ds(pl.multiple_of(r * quarter, quarter), quarter)
    diagonal = []
    for k in (1, 2, 3):
        diagonal.append(remote(dg.at[:, strip], dq.at[c], 7 + k, col_peer(k)))
    dq[c] = dg[:, strip, :]

    rotate(far_other)
    crossing.append(remote(w.at[hx, chunk(far_other)], got.at[c, hx], 4, {"col": far_other}))
    near = [remote(w.at[ho, chunk(far_other)], ex.at[odd], 7, {"col": partner})]
    rotate(partner)
    near.append(remote(w.at[hx, chunk(partner)], got.at[c, hx], 5, {"col": partner}))
    near.append(remote(w.at[ho, chunk(partner)], got.at[c, ho], 6, {"col": partner}))

    rotate(c)
    got[c, 0] = w[0, chunk(c), :]
    got[c, 1] = w[1, chunk(c), :]
    ex[odd] = w[ho, chunk(far), :]

    def later(part_of, sem):
        size = rows // 2
        sent = []
        for i, j in enumerate((far, far_other)):
            at = pl.ds(pl.multiple_of(j * rows + part_of * size, size), size)
            to = pl.ds(part_of * size, size)
            sent.append(remote(w.at[ho, at], got.at[c, ho, to], sem + i, {"col": j}))
        return sent

    second = later(0, 14)

    for copy in diagonal:
        copy.wait()
    for k in (1, 2, 3):
        diagonal.append(remote(dq, df.at[r], 10 + k, row_peer(k)))
    df[r] = dq[...]
    for copy in diagonal[3:]:
        copy.wait()
    for copy in crossing:
        copy.wait()
    for copy in near:
        copy.wait()

    def cross(left, right):
        return split_dot(halves_of(left), halves_of(right), ROWS_FIRST)

    left_col = 2 * side
    part[...] = jnp.zeros_like(part)

    @pl.loop(0, rows // piece_rows)
    def _(t):
        at = pl.ds(pl.multiple_of(t * piece_rows, piece_rows), piece_rows)
        part[0] += cross(got[0, 1, at, :], got[2, 1, at, :])
        part[1] += cross(got[1, 0, at, :], got[3, 1, at, :])
        part[2] += cross(got[left_col, 0, at, :], got[left_col + 1, 1 - side, at, :])
        part[2] += cross(ex[0, at, :], ex[1, at, :])

    copies = []
    for k in (1, 2, 3):
        q = lax.rem(r + k, n_row)
        theirs = pl.ds(pl.multiple_of(q * quarter, quarter), quarter)
        copies.append(remote(part.at[:, theirs], rs.at[k - 1], 15 + k, {"row": q}))
    for copy in copies:
        copy.wait()
    zb[c] = (part[:, strip, :] + rs[0]) + (rs[1] + rs[2])
    copies = [remote(zb.at[c], zb.at[c], 18 + k, col_peer(k)) for k in (1, 2, 3)]
    second += later(1, 25)
    for copy in copies:
        copy.wait()
    cq[0] = zb[0, 2] + zb[1, 2]
    cq[1] = (zb[0, 0] + zb[1, 0]) + (zb[2, 0] + zb[3, 0])
    cq[2] = (zb[0, 1] + zb[1, 1]) + (zb[2, 1] + zb[3, 1])
    cq[3] = zb[2, 2] + zb[3, 2]
    copies = [remote(cq, cf.at[r], 21 + k, row_peer(k)) for k in (1, 2, 3)]
    cf[r] = cq[...]
    for copy in copies:
        copy.wait()

    for slot, ((lc, lh), (rc, rh)) in enumerate(SLOTS):
        for q in range(n_row):
            at = slice(q * quarter, (q + 1) * quarter)
            low = slice(half + q * quarter, half + (q + 1) * quarter)
            y2[slot, at, :half] = df[q, lc, lh]
            y2[slot, low, half:] = df[q, rc, rh]
            y2[slot, at, half:] = cf[q, slot]
        y2[slot, half:, :half] = jnp.transpose(y2[slot, :half, half:])

    factors = []
    for i in range(2):
        gram = y2[2 * core + i]
        norm = norm_of(gram)
        y2[2 * core + i] = gram / norm
        factors.append(jnp.sqrt(total_rows / norm))
    own = pl.ds(2 * core, 2)
    newton(y2.at[own], z2.at[own], 2)
    for i in range(2):
        z2[2 * core + i] = z2[2 * core + i] * factors[i]
    copy = remote(z2.at[own], z2.at[own], 27, core_peer)
    copy.wait()

    def finish(slot):
        (lc, lh), (rc, rh) = SLOTS[slot]

        @pl.loop(0, rows // piece_rows)
        def _(t):
            at = pl.ds(pl.multiple_of(t * piece_rows, piece_rows), piece_rows)
            both = jnp.concatenate([got[lc, lh, at, :], got[rc, rh, at, :]], axis=1)
            turned = split_dot(halves_of(both), halves_of(z2[slot]))
            for side_of in range(2):
                place = PLACES[slot][side_of]
                out_ref[at, place * half:(place + 1) * half] = turned[:, side_of * half:(side_of + 1) * half]

    finish(1)
    finish(2)
    for copy in second:
        copy.wait()
    finish(0)
    finish(3)


def fused(records):
    slab, width = records.shape
    half = width // 2
    rows = slab // 4
    quarter = half // 4
    out = pl.pallas_call(
        kernel,
        out_shape=jax.ShapeDtypeStruct((rows, 4 * width), F32),
        in_specs=[pl.BlockSpec(memory_space=pl.ANY)],
        out_specs=pl.BlockSpec(memory_space=pltpu.VMEM),
        scratch_shapes=[
            pltpu.VMEM((slab, width), F32),
            pltpu.VMEM((2, slab, half), F32),
            pltpu.VMEM((4, 2, rows, half), F32),
            pltpu.VMEM((2, rows, half), F32),
            pltpu.VMEM((width, width), F32),
            pltpu.VMEM((half, width), F32),
            pltpu.VMEM((half, width), F32),
            pltpu.VMEM((half, width), F32),
            pltpu.VMEM((width, width), F32),
            pltpu.VMEM((1, width, width), F32),
            pltpu.VMEM((1, width, width), F32),
            pltpu.VMEM((2, half, half), F32),
            pltpu.VMEM((4, 2, quarter, half), F32),
            pltpu.VMEM((4, 4, 2, quarter, half), F32),
            pltpu.VMEM((3, half, half), F32),
            pltpu.VMEM((3, 3, quarter, half), F32),
            pltpu.VMEM((4, 3, quarter, half), F32),
            pltpu.VMEM((4, quarter, half), F32),
            pltpu.VMEM((4, 4, quarter, half), F32),
            pltpu.VMEM((4, width, width), F32),
            pltpu.VMEM((4, width, width), F32),
            pltpu.SemaphoreType.DMA((28,)),
            pltpu.SemaphoreType.DMA((28,)),
            pltpu.SemaphoreType.DMA((8,)),
        ],
        compiler_params=pltpu.CompilerParams(
            collective_id=0, has_side_effects=True, vmem_limit_bytes=48 * 1024 * 1024),
    )(records)
    return out.reshape(1, rows, 4 * width)


def shifted(x, axis, by):
    peers = lax.axis_size(axis)
    pairs = [(i, i + by) for i in range(peers) if 0 <= i + by < peers]
    return lax.ppermute(x, axis, pairs)


def local_gram(left, right):
    return lax.dot_general(
        left, right, ROWS_FIRST, precision=lax.Precision.HIGHEST, preferred_element_type=F32)


def inverse_root(gram_pair):
    identity = jnp.eye(gram_pair.shape[0], dtype=F32)
    norm_total = jnp.sqrt(jnp.sum(gram_pair * gram_pair) + 1e-06)
    root_part = gram_pair / norm_total
    inverse_part = identity
    for repeat in range(NS_ITERS):
        middle = 1.5 * identity - 0.5 * exact_dot(inverse_part, root_part)
        root_part = exact_dot(root_part, middle)
        inverse_part = exact_dot(middle, inverse_part)
    return (inverse_part, norm_total)


def stepwise(records):
    col_count = lax.axis_size("col")
    total_rows = records.shape[0] * lax.axis_size("row")
    position = lax.axis_index("col")
    first_col = position == 0
    last_col = position == col_count - 1
    block_width = records.shape[1] // 2
    pair_cols = records
    for repeat in range(TOURS):
        gram_pair = lax.psum(local_gram(pair_cols, pair_cols), "row")
        inverse_part, norm_total = inverse_root(gram_pair)
        factor = jnp.sqrt(total_rows / norm_total)
        pair_cols = exact_dot(pair_cols, inverse_part) * factor
        top_block = pair_cols[:, :block_width]
        bottom_block = pair_cols[:, block_width:]
        outgoing = jnp.where(first_col, bottom_block, top_block)
        arrived = shifted(outgoing, "col", 1)
        returned = shifted(bottom_block, "col", -1)
        new_bottom = jnp.where(last_col, top_block, returned)
        top_block = jnp.where(first_col, top_block, arrived)
        pair_cols = jnp.concatenate([top_block, new_bottom], axis=1)
    spread = lax.all_to_all(pair_cols, "col", split_axis=0, concat_axis=1, tiled=True)
    return spread.reshape(1, spread.shape[0], spread.shape[1])


def solution(mesh):
    placed = (P(("grp", "row"), "col"),)
    small = mesh.shape["col"] == 4 and mesh.shape["row"] == 4
    return jax.shard_map(
        fused if small else stepwise,
        mesh=mesh, in_specs=placed, out_specs=P(("grp", "row"), "col", None), check_vma=False
    )
```

```python
import jax
import jax.numpy as jnp
from jax import lax
from jax.experimental import pallas as pl
from jax.experimental.pallas import tpu as pltpu
from jax.sharding import PartitionSpec as P

NS_ITERS = 8
TOURS = 2
MESH = pl.DeviceIdType.MESH
F32 = jnp.float32
BF16 = jnp.bfloat16
ROWS_FIRST = (((0,), (0,)), ((), ()))
PLAIN = (((1,), (0,)), ((), ()))
SLOTS = (((0, 0), (1, 1)), ((0, 1), (2, 1)), ((1, 0), (3, 1)), ((2, 0), (3, 0)))
PLACES = ((0, 2), (4, 1), (6, 3), (7, 5))


def exact_dot(left, right):
    return jnp.dot(left, right, precision=lax.Precision.HIGHEST, preferred_element_type=F32)


def halves_of(value):
    high = value.astype(BF16)
    low = (value - high.astype(F32)).astype(BF16)
    return high, low


def split_dot(left, right, dims=PLAIN):
    left_high, left_low = left
    right_high, right_low = right

    def one(a, b):
        return lax.dot_general(a, b, dims, preferred_element_type=F32)

    return one(left_high, right_high) + (one(left_high, right_low) + one(left_low, right_high))


def identity_of(width):
    rows = lax.broadcasted_iota(jnp.int32, (width, width), 0)
    cols = lax.broadcasted_iota(jnp.int32, (width, width), 1)
    return jnp.where(rows == cols, 1.0, 0.0).astype(F32)


def norm_of(gram):
    total = jnp.sum(jnp.sum(gram * gram, axis=1, keepdims=True), axis=0, keepdims=True)
    return jnp.sqrt(total + 1e-06)


def newton(y_ref, z_ref, count):
    width = y_ref.shape[1]
    identity = identity_of(width)
    for i in range(count):
        middle = 1.5 * identity - 0.5 * y_ref[i]
        y_ref[i] = exact_dot(y_ref[i], middle)
        z_ref[i] = middle

    @pl.loop(1, NS_ITERS - 1)
    def _(step):
        middles = []
        for i in range(count):
            middles.append(1.5 * identity - 0.5 * exact_dot(z_ref[i], y_ref[i]))
        for i in range(count):
            y_ref[i] = exact_dot(y_ref[i], middles[i])
            z_ref[i] = exact_dot(middles[i], z_ref[i])

    for i in range(count):
        middle = 1.5 * identity - 0.5 * exact_dot(z_ref[i], y_ref[i])
        z_ref[i] = exact_dot(middle, z_ref[i])


def kernel(x_any, out_ref, x_ref, w, got, ex, g, ga, sb, gb, gf, y1, z1, dg, dq, df, part, rs, zb, cq, cf, y2, z2,
           send_sem, recv_sem, load_sem):
    n_col, n_row = 4, 4
    c = lax.axis_index("col")
    r = lax.axis_index("row")
    slab, width = x_ref.shape
    half = width // 2
    rows = slab // n_col
    quarter = half // n_row
    total_rows = float(slab * n_row)

    def col_peer(k):
        return {"col": lax.rem(c + k, n_col)}

    def row_peer(k):
        return {"row": lax.rem(r + k, n_row)}

    def remote(src, dst, sem, device):
        copy = pltpu.make_async_remote_copy(
            src_ref=src, dst_ref=dst, send_sem=send_sem.at[sem], recv_sem=recv_sem.at[sem],
            device_id=device, device_id_type=MESH)
        copy.start()
        return copy

    tile = slab // 8

    def load(t):
        at = pl.ds(pl.multiple_of(t * tile, tile), tile)
        return pltpu.make_async_copy(x_any.at[at], x_ref.at[at], load_sem.at[t])

    for t in range(8):
        load(t).start()

    barrier = pltpu.get_barrier_semaphore()
    for k in range(1, n_row):
        pl.semaphore_signal(barrier, inc=1, device_id=row_peer(k), device_id_type=MESH)
    for k in range(1, n_col):
        pl.semaphore_signal(barrier, inc=1, device_id=col_peer(k), device_id_type=MESH)

    g[...] = jnp.zeros_like(g)
    gf[...] = jnp.zeros_like(gf)

    @pl.loop(0, slab // tile)
    def _(t):
        load(t).wait()
        piece = halves_of(x_ref[pl.ds(pl.multiple_of(t * tile, tile), tile), :])
        g[...] += lax.dot_general(piece[0], piece[0], ROWS_FIRST, preferred_element_type=F32)
        gf[...] += lax.dot_general(piece[0], piece[1], ROWS_FIRST, preferred_element_type=F32)

    g[...] += gf[...] + jnp.transpose(gf[...])

    pl.semaphore_wait(barrier, n_row + n_col - 2)

    core = lax.rem(r, 2)
    mine = pl.ds(pl.multiple_of(core * half, half), half)
    other = pl.ds(pl.multiple_of((1 - core) * half, half), half)
    core_peer = {"row": r + 1 - 2 * core}
    copy = remote(g.at[other], ga, 0, core_peer)
    copy.wait()
    sb[...] = g[mine, :] + ga[...]
    copy = remote(sb, gb, 1, row_peer(2))
    copy.wait()
    gf[mine, :] = sb[...] + gb[...]
    copy = remote(gf.at[mine], gf.at[mine], 2, core_peer)
    copy.wait()

    norm = norm_of(gf[...])
    y1[0] = gf[...] / norm
    newton(y1, z1, 1)
    z1[0] = z1[0] * jnp.sqrt(total_rows / norm)

    odd = lax.rem(c, 2)
    side = c // 2
    hx = 1 - odd * (1 - side)
    ho = 1 - hx
    partner = c + 1 - 2 * odd
    far = lax.rem(c + 2, n_col)
    far_other = lax.rem(partner + 2, n_col)

    def chunk(j):
        return pl.ds(pl.multiple_of(j * rows, rows), rows)

    piece_rows = min(256, rows)

    def rotate(j):
        @pl.loop(0, rows // piece_rows)
        def _(t):
            at = pl.ds(pl.multiple_of(j * rows + t * piece_rows, piece_rows), piece_rows)
            turned = split_dot(halves_of(x_ref[at, :]), halves_of(z1[0]))
            w[0, at, :] = turned[:, :half]
            w[1, at, :] = turned[:, half:]

    rotate(far)
    crossing = [remote(w.at[hx, chunk(far)], got.at[c, hx], 3, {"col": far})]

    turned_gram = exact_dot(exact_dot(z1[0], gf[...]), z1[0])
    dg[0] = turned_gram[:half, :half]
    dg[1] = turned_gram[half:, half:]
    strip = pl.ds(pl.multiple_of(r * quarter, quarter), quarter)
    diagonal = []
    for k in (1, 2, 3):
        diagonal.append(remote(dg.at[:, strip], dq.at[c], 7 + k, col_peer(k)))
    dq[c] = dg[:, strip, :]

    rotate(far_other)
    crossing.append(remote(w.at[hx, chunk(far_other)], got.at[c, hx], 4, {"col": far_other}))
    near = [remote(w.at[ho, chunk(far_other)], ex.at[odd], 7, {"col": partner})]
    rotate(partner)
    near.append(remote(w.at[hx, chunk(partner)], got.at[c, hx], 5, {"col": partner}))
    near.append(remote(w.at[ho, chunk(partner)], got.at[c, ho], 6, {"col": partner}))

    rotate(c)
    got[c, 0] = w[0, chunk(c), :]
    got[c, 1] = w[1, chunk(c), :]
    ex[odd] = w[ho, chunk(far), :]

    def later(part_of, sem):
        size = rows // 2
        sent = []
        for i, j in enumerate((far, far_other)):
            at = pl.ds(pl.multiple_of(j * rows + part_of * size, size), size)
            to = pl.ds(part_of * size, size)
            sent.append(remote(w.at[ho, at], got.at[c, ho, to], sem + i, {"col": j}))
        return sent

    for copy in crossing:
        copy.wait_send()
    second = later(0, 14)

    for copy in diagonal:
        copy.wait()
    for k in (1, 2, 3):
        diagonal.append(remote(dq, df.at[r], 10 + k, row_peer(k)))
    df[r] = dq[...]
    for copy in diagonal[3:]:
        copy.wait()
    for copy in crossing:
        copy.wait_recv()
    for copy in near:
        copy.wait()

    def cross(left, right):
        return split_dot(halves_of(left), halves_of(right), ROWS_FIRST)

    left_col = 2 * side
    part[...] = jnp.zeros_like(part)

    @pl.loop(0, rows // piece_rows)
    def _(t):
        at = pl.ds(pl.multiple_of(t * piece_rows, piece_rows), piece_rows)
        part[0] += cross(got[0, 1, at, :], got[2, 1, at, :])
        part[1] += cross(got[1, 0, at, :], got[3, 1, at, :])
        part[2] += cross(got[left_col, 0, at, :], got[left_col + 1, 1 - side, at, :])
        part[2] += cross(ex[0, at, :], ex[1, at, :])

    copies = []
    for k in (1, 2, 3):
        q = lax.rem(r + k, n_row)
        theirs = pl.ds(pl.multiple_of(q * quarter, quarter), quarter)
        copies.append(remote(part.at[:, theirs], rs.at[k - 1], 15 + k, {"row": q}))
    for copy in copies:
        copy.wait()
    zb[c] = (part[:, strip, :] + rs[0]) + (rs[1] + rs[2])
    copies = [remote(zb.at[c], zb.at[c], 18 + k, col_peer(k)) for k in (1, 2, 3)]
    second += later(1, 25)
    for copy in copies:
        copy.wait()
    cq[0] = zb[0, 2] + zb[1, 2]
    cq[1] = (zb[0, 0] + zb[1, 0]) + (zb[2, 0] + zb[3, 0])
    cq[2] = (zb[0, 1] + zb[1, 1]) + (zb[2, 1] + zb[3, 1])
    cq[3] = zb[2, 2] + zb[3, 2]
    copies = [remote(cq, cf.at[r], 21 + k, row_peer(k)) for k in (1, 2, 3)]
    cf[r] = cq[...]
    for copy in copies:
        copy.wait()

    for slot, ((lc, lh), (rc, rh)) in enumerate(SLOTS):
        for q in range(n_row):
            at = slice(q * quarter, (q + 1) * quarter)
            low = slice(half + q * quarter, half + (q + 1) * quarter)
            y2[slot, at, :half] = df[q, lc, lh]
            y2[slot, low, half:] = df[q, rc, rh]
            y2[slot, at, half:] = cf[q, slot]
        y2[slot, half:, :half] = jnp.transpose(y2[slot, :half, half:])

    factors = []
    for i in range(2):
        gram = y2[2 * core + i]
        norm = norm_of(gram)
        y2[2 * core + i] = gram / norm
        factors.append(jnp.sqrt(total_rows / norm))
    own = pl.ds(2 * core, 2)
    newton(y2.at[own], z2.at[own], 2)
    for i in range(2):
        z2[2 * core + i] = z2[2 * core + i] * factors[i]
    copy = remote(z2.at[own], z2.at[own], 27, core_peer)
    copy.wait()

    def finish(slot):
        (lc, lh), (rc, rh) = SLOTS[slot]

        @pl.loop(0, rows // piece_rows)
        def _(t):
            at = pl.ds(pl.multiple_of(t * piece_rows, piece_rows), piece_rows)
            both = jnp.concatenate([got[lc, lh, at, :], got[rc, rh, at, :]], axis=1)
            turned = split_dot(halves_of(both), halves_of(z2[slot]))
            for side_of in range(2):
                place = PLACES[slot][side_of]
                out_ref[at, place * half:(place + 1) * half] = turned[:, side_of * half:(side_of + 1) * half]

    finish(1)
    finish(2)
    for copy in second:
        copy.wait()
    finish(0)
    finish(3)


def fused(records):
    slab, width = records.shape
    half = width // 2
    rows = slab // 4
    quarter = half // 4
    out = pl.pallas_call(
        kernel,
        out_shape=jax.ShapeDtypeStruct((rows, 4 * width), F32),
        in_specs=[pl.BlockSpec(memory_space=pl.ANY)],
        out_specs=pl.BlockSpec(memory_space=pltpu.VMEM),
        scratch_shapes=[
            pltpu.VMEM((slab, width), F32),
            pltpu.VMEM((2, slab, half), F32),
            pltpu.VMEM((4, 2, rows, half), F32),
            pltpu.VMEM((2, rows, half), F32),
            pltpu.VMEM((width, width), F32),
            pltpu.VMEM((half, width), F32),
            pltpu.VMEM((half, width), F32),
            pltpu.VMEM((half, width), F32),
            pltpu.VMEM((width, width), F32),
            pltpu.VMEM((1, width, width), F32),
            pltpu.VMEM((1, width, width), F32),
            pltpu.VMEM((2, half, half), F32),
            pltpu.VMEM((4, 2, quarter, half), F32),
            pltpu.VMEM((4, 4, 2, quarter, half), F32),
            pltpu.VMEM((3, half, half), F32),
            pltpu.VMEM((3, 3, quarter, half), F32),
            pltpu.VMEM((4, 3, quarter, half), F32),
            pltpu.VMEM((4, quarter, half), F32),
            pltpu.VMEM((4, 4, quarter, half), F32),
            pltpu.VMEM((4, width, width), F32),
            pltpu.VMEM((4, width, width), F32),
            pltpu.SemaphoreType.DMA((28,)),
            pltpu.SemaphoreType.DMA((28,)),
            pltpu.SemaphoreType.DMA((8,)),
        ],
        compiler_params=pltpu.CompilerParams(
            collective_id=0, has_side_effects=True, vmem_limit_bytes=48 * 1024 * 1024),
    )(records)
    return out.reshape(1, rows, 4 * width)


def shifted(x, axis, by):
    peers = lax.axis_size(axis)
    pairs = [(i, i + by) for i in range(peers) if 0 <= i + by < peers]
    return lax.ppermute(x, axis, pairs)


def local_gram(left, right):
    return lax.dot_general(
        left, right, ROWS_FIRST, precision=lax.Precision.HIGHEST, preferred_element_type=F32)


def inverse_root(gram_pair):
    identity = jnp.eye(gram_pair.shape[0], dtype=F32)
    norm_total = jnp.sqrt(jnp.sum(gram_pair * gram_pair) + 1e-06)
    root_part = gram_pair / norm_total
    inverse_part = identity
    for repeat in range(NS_ITERS):
        middle = 1.5 * identity - 0.5 * exact_dot(inverse_part, root_part)
        root_part = exact_dot(root_part, middle)
        inverse_part = exact_dot(middle, inverse_part)
    return (inverse_part, norm_total)


def stepwise(records):
    col_count = lax.axis_size("col")
    total_rows = records.shape[0] * lax.axis_size("row")
    position = lax.axis_index("col")
    first_col = position == 0
    last_col = position == col_count - 1
    block_width = records.shape[1] // 2
    pair_cols = records
    for repeat in range(TOURS):
        gram_pair = lax.psum(local_gram(pair_cols, pair_cols), "row")
        inverse_part, norm_total = inverse_root(gram_pair)
        factor = jnp.sqrt(total_rows / norm_total)
        pair_cols = exact_dot(pair_cols, inverse_part) * factor
        top_block = pair_cols[:, :block_width]
        bottom_block = pair_cols[:, block_width:]
        outgoing = jnp.where(first_col, bottom_block, top_block)
        arrived = shifted(outgoing, "col", 1)
        returned = shifted(bottom_block, "col", -1)
        new_bottom = jnp.where(last_col, top_block, returned)
        top_block = jnp.where(first_col, top_block, arrived)
        pair_cols = jnp.concatenate([top_block, new_bottom], axis=1)
    spread = lax.all_to_all(pair_cols, "col", split_axis=0, concat_axis=1, tiled=True)
    return spread.reshape(1, spread.shape[0], spread.shape[1])


def solution(mesh):
    placed = (P(("grp", "row"), "col"),)
    small = mesh.shape["col"] == 4 and mesh.shape["row"] == 4
    return jax.shard_map(
        fused if small else stepwise,
        mesh=mesh, in_specs=placed, out_specs=P(("grp", "row"), "col", None), check_vma=False
    )
```
